32 devices in a mesh: gx: 4 (over z), gy: 4 (over x, core), sa: 2 (over y).
Axes of the slice: x: 2, y: 2, z: 4, core: 2. Of those that a mesh axis runs over, the one named last changes fastest.
Arguments:
- right_side: float32 [64, 256, 256], P('gx', 'gy', 'sa'), may hold values from -8 to 8
- diagonal: float32 [64, 256, 256], P('gx', 'gy', 'sa'), may hold values from 0.25 to 2
Outputs:
- pressure: float32 [64, 256, 256], P('gx', 'gy', 'sa')
- residual: float32 [64, 256, 256], P('gx', 'gy', 'sa')
The draws below stay inside these ranges and needn't reach their ends.
All inputs are finite; a program needn't handle non-finite values.
Results may differ from the reference program's by a relative error of at most 0.0001.
Values sent between devices are 32-bit elements; how exact they have to be, the bound alone decides.
A program may use at most 192 MiB of HBM per device.

```python
import jax
import jax.numpy as jnp

CYCLES = 2
SWEEPS = 5
COARSE_SWEEPS = 6
NX = 64
NY = 256
NZ = 256


def level_of(key, extent, cuts, least, top_value):
    def one(dim, parts):
        heights = jax.random.uniform(jax.random.fold_in(jax.random.fold_in(key, 6), dim), (parts,), jnp.float32, least / len(cuts), top_value / len(cuts))
        return jnp.repeat(jnp.exp(heights), extent[dim] // parts).reshape((-1,) + (1,) * (len(extent) - dim - 1))

    level = one(*cuts[0])
    for cut in cuts[1:]:
        level = level * one(*cut)
    return level


def normal_values(rng, shape, deviation, bound, cuts=(), kind=jnp.bfloat16):
    loudness = level_of(rng, shape, cuts, -0.22, 0.18) if cuts else 1.0
    values = jax.random.normal(rng, shape, jnp.float32) * deviation * loudness
    return jnp.minimum(jnp.maximum(values, -bound), bound).astype(kind)


def setup_inputs(seed: int = 0) -> dict:
    streams_of = jax.random.split(jax.random.key(seed), 3)
    right_side = normal_values(streams_of[0], (NX, NY, NZ), 1.0, 8.0, ((0, 4), (1, 4), (2, 2)), jnp.float32)
    diagonal = jnp.clip(0.25 + 1.75 * jax.random.uniform(streams_of[1], (NX, NY, NZ), jnp.float32) ** level_of(streams_of[1], (NX, NY, NZ), ((0, 4), (1, 4), (2, 2)), -0.2, 0.2), 0.25, 2.0)
    return dict(right_side=right_side, diagonal=diagonal)


damping = 2.0 / 3.0


def beside_sum(padded):
    total = padded[2:, 1:-1, 1:-1] + padded[:-2, 1:-1, 1:-1]
    total = total + padded[1:-1, 2:, 1:-1] + padded[1:-1, :-2, 1:-1]
    total = total + padded[1:-1, 1:-1, 2:] + padded[1:-1, 1:-1, :-2]
    return total


def operate(field, diag_field):
    return (6.0 + diag_field) * field - beside_sum(jnp.pad(field, 1))


def restrict(field):
    sx, sy, sz = field.shape
    return field.reshape(sx // 2, 2, sy // 2, 2, sz // 2, 2).sum(axis=(1, 3, 5)) * 0.5


def prolong(field):
    sx, sy, sz = field.shape
    wide = jnp.broadcast_to(field[:, None, :, None, :, None], (sx, 2, sy, 2, sz, 2))
    return wide.reshape(2 * sx, 2 * sy, 2 * sz)


def smooth(source, diag_field, count):
    correction = damping * source / (6.0 + diag_field)
    for sweep in range(count - 1):
        correction = correction + damping * (source - operate(correction, diag_field)) / (6.0 + diag_field)
    return correction


def reference(right_side, diagonal):
    coarse_diagonal = restrict(diagonal)
    pressure = jnp.zeros_like(right_side)
    rest = right_side
    for cycle in range(CYCLES):
        if cycle > 0:
            rest = right_side - operate(pressure, diagonal)
        fine_part = smooth(rest, diagonal, SWEEPS)
        coarse_part = smooth(restrict(rest), coarse_diagonal, COARSE_SWEEPS)
        pressure = pressure + fine_part + prolong(coarse_part)
    residual = right_side - operate(pressure, diagonal)
    return pressure, residual
```

```python
import functools

import jax
import jax.numpy as jnp
from jax import lax
from jax.experimental import pallas as pl
from jax.experimental.pallas import tpu as pltpu
from jax.sharding import PartitionSpec as P

CYCLES = 2
SWEEPS = 5
COARSE_SWEEPS = 6
W = 2.0 / 3.0
AXES = ("gx", "gy", "sa")
MESH = pl.DeviceIdType.MESH
S = 8
L = 128


class Level:
    def __init__(self, nx, nj, dz, refs):
        self.nx, self.nj, self.dz = nx, nj, dz
        self.E, self.F, self.G, self.YS, self.YR, self.ZS, self.ZR, self.ssem, self.rsem = refs


def scratch_of(nx, nj):
    return [
        pltpu.VMEM((2, nx + 2, nj, S, L), jnp.float32),
        pltpu.VMEM((nx, nj, S, L), jnp.float32),
        pltpu.VMEM((nx, nj, S, L), jnp.float32),
        pltpu.VMEM((2, 2, nx, L), jnp.float32),
        pltpu.VMEM((2, 2, nx, L), jnp.float32),
        pltpu.VMEM((2, S, L), jnp.float32),
        pltpu.VMEM((2, S, L), jnp.float32),
        pltpu.SemaphoreType.DMA((2, 5)),
        pltpu.SemaphoreType.DMA((2, 5)),
    ]


def kernel(sizes, nx, nj, f_ref, d_ref, p_ref, r_ref, *scratch):
    fine = Level(nx, nj, 1, scratch[0:9])
    coarse = Level(nx // 2, nj // 2, 2, scratch[9:18])
    PB = scratch[18]
    gx, gy, sa = (lax.axis_index(a) for a in AXES)
    ngx, ngy, _ = sizes
    has = [gx > 0, gx < ngx - 1, gy > 0, gy < ngy - 1, None]
    to = [
        (gx - 1, gy, sa),
        (gx + 1, gy, sa),
        (gx, gy - 1, sa),
        (gx, gy + 1, sa),
        (gx, gy, 1 - sa),
    ]

    lane = lax.broadcasted_iota(jnp.int32, (S, L), 1)
    row = lax.broadcasted_iota(jnp.int32, (S, L), 0)
    even = lane % 2 == 0
    zero = jnp.zeros((S, L), jnp.float32)

    def when(cond, fn):
        if cond is None:
            fn()
        else:
            pl.when(cond)(fn)

    def copies(lv, slot):
        pairs = [
            (lv.E.at[slot, 1], lv.E.at[slot, lv.nx + 1]),
            (lv.E.at[slot, lv.nx], lv.E.at[slot, 0]),
            (lv.YS.at[slot, 0], lv.YR.at[slot, 1]),
            (lv.YS.at[slot, 1], lv.YR.at[slot, 0]),
            (lv.ZS.at[slot], lv.ZR.at[slot]),
        ]
        back = [1, 0, 3, 2, 4]
        return [
            pltpu.make_async_remote_copy(
                src_ref=a,
                dst_ref=b,
                send_sem=lv.ssem.at[slot, i],
                recv_sem=lv.rsem.at[slot, back[i]],
                device_id=to[i],
                device_id_type=MESH,
            )
            for i, (a, b) in enumerate(pairs)
        ]

    def arrivals(lv, slot):
        cs = copies(lv, slot)
        return [cs[1], cs[0], cs[3], cs[2], cs[4]]

    def send(lv, slot):
        cs = copies(lv, slot)
        for i in range(5):
            when(has[i], cs[i].start)

    def wait(lv, slot):
        cs = copies(lv, slot)
        ar = arrivals(lv, slot)
        for i in range(5):
            def both(i=i):
                cs[i].wait_send()
                ar[i].wait_recv()

            when(has[i], both)

    def face(lv):
        base = jnp.where(sa == 0, L - lv.dz, 0)
        return lax.rem(lane - base + L, L) // lv.dz

    def put(lv, slot, x, tiles, acc):
        rel = face(lv)
        for j, t in enumerate(tiles):
            lv.E[slot, x + 1, j] = t
            moved = t if j == 0 else pltpu.roll(t, lv.dz * j, 1)
            acc = jnp.where(rel == j, moved, acc)
        lv.YS[slot, 0, pl.ds(x, 1), :] = tiles[0][0:1]
        lv.YS[slot, 1, pl.ds(x, 1), :] = tiles[-1][S - 1 : S]
        return pltpu.roll(acc, L - lv.dz * lv.nj, 1)

    def put_end(lv, slot, acc):
        over = (lv.nx * lv.nj * lv.dz) % L
        lv.ZS[slot] = acc if over == 0 else pltpu.roll(acc, over, 1)

    def face_start(lv, slot):
        z = lv.ZR[slot]
        return jnp.where(sa == 0, pltpu.roll(z, L - lv.dz, 1), pltpu.roll(z, lv.dz, 1))

    def around(lv, slot, x, halo):
        nj, dz = lv.nj, lv.dz
        mine = face(lv) == 0
        c = [lv.E[slot, x + 1, j] for j in range(nj)]
        below = jnp.where(row == 0, lv.YR[slot, 0, pl.ds(x, 1), :], pltpu.roll(c[-1], 1, 0))
        above = jnp.where(row == S - 1, lv.YR[slot, 1, pl.ds(x, 1), :], pltpu.roll(c[0], S - 1, 0))
        ext = [below] + c + [above]
        sums = []
        for j in range(nj):
            t = lv.E[slot, x, j] + lv.E[slot, x + 2, j] + (ext[j] + ext[j + 2])
            zl = jnp.where(lane < dz, 0.0, pltpu.roll(c[j], dz, 1))
            zr = jnp.where(lane >= L - dz, 0.0, pltpu.roll(c[j], L - dz, 1))
            h = halo if j == 0 else pltpu.roll(halo, L - dz * j, 1)
            sums.append(t + (zl + zr) + jnp.where(mine, h, 0.0))
        return c, sums, pltpu.roll(halo, L - dz * nj, 1)

    def sweep(lv, src, last):
        dst = 1 - src

        def plane(x, carry):
            halo, acc = carry
            c, sums, halo = around(lv, src, x, halo)
            new = [
                (1.0 - W) * c[j] + lv.G[x, j] * (lv.F[x, j] + sums[j]) for j in range(lv.nj)
            ]
            if last:
                for j in range(lv.nj):
                    lv.E[dst, x + 1, j] = new[j]
            else:
                acc = put(lv, dst, x, new, acc)
            return halo, acc

        _, acc = lax.fori_loop(0, lv.nx, plane, (face_start(lv, src), zero))
        if not last:
            put_end(lv, dst, acc)

    def restrict(tiles):
        t = (tiles[0] + tiles[1]) + (tiles[2] + tiles[3])
        return 0.5 * (t + jnp.where(even, pltpu.roll(t, L - 1, 1), pltpu.roll(t, 1, 1)))

    def begin(slot, first):
        def plane(X, carry):
            facc, cacc = carry
            f = [[None] * nj, [None] * nj]
            d = [[None] * nj, [None] * nj]
            for i in range(2):
                x = 2 * X + i
                for j in range(nj):
                    if first:
                        f[i][j] = f_ref[x, pl.ds(j, S, stride=nj), :]
                        fine.F[x, j] = f[i][j]
                        d[i][j] = d_ref[x, pl.ds(j, S, stride=nj), :]
                        fine.G[x, j] = W / (6.0 + d[i][j])
                    else:
                        f[i][j] = fine.F[x, j]
                facc = put(
                    fine, slot, x, [fine.G[x, j] * f[i][j] for j in range(nj)], facc
                )
            new = []
            for J in range(nj // 2):
                cf = restrict([f[i][2 * J + k] for i in range(2) for k in range(2)])
                coarse.F[X, J] = cf
                if first:
                    cd = restrict([d[i][2 * J + k] for i in range(2) for k in range(2)])
                    coarse.G[X, J] = W / (6.0 + cd)
                new.append(coarse.G[X, J] * cf)
            return facc, put(coarse, slot, X, new, cacc)

        facc, cacc = lax.fori_loop(0, nx // 2, plane, (zero, zero))
        put_end(fine, slot, facc)
        put_end(coarse, slot, cacc)

    for lv in (fine, coarse):
        for slot in range(2):
            for plane in (0, lv.nx + 1):
                lv.E[slot, plane] = jnp.zeros((lv.nj, S, L), jnp.float32)
            lv.YR[slot] = jnp.zeros((2, lv.nx, L), jnp.float32)

    barrier = pltpu.get_barrier_semaphore()
    for i in range(5):
        def hello(i=i):
            pl.semaphore_signal(barrier, inc=1, device_id=to[i], device_id_type=MESH)

        when(has[i], hello)
    count = 1 + sum(h.astype(jnp.int32) for h in has[:4])
    pl.semaphore_wait(barrier, count)

    slot = 0
    for cycle in range(CYCLES):
        begin(slot, cycle == 0)
        send(fine, slot)
        send(coarse, slot)
        fs = cs = slot
        for step in range(max(SWEEPS, COARSE_SWEEPS) - 1):
            if step < SWEEPS - 1:
                last = step == SWEEPS - 2
                wait(fine, fs)
                sweep(fine, fs, last)
                fs = 1 - fs
                if not last:
                    send(fine, fs)
            if step < COARSE_SWEEPS - 1:
                last = step == COARSE_SWEEPS - 2
                wait(coarse, cs)
                sweep(coarse, cs, last)
                cs = 1 - cs
                if not last:
                    send(coarse, cs)

        def add(X, acc):
            for i in range(2):
                x = 2 * X + i
                tiles = []
                for j in range(nj):
                    t = fine.E[fs, x + 1, j] + coarse.E[cs, X + 1, j // 2]
                    if cycle > 0:
                        t = t + PB[x, j]
                    if cycle < CYCLES - 1:
                        PB[x, j] = t
                    else:
                        p_ref[x, pl.ds(j, S, stride=nj), :] = t
                    tiles.append(t)
                acc = put(fine, fs, x, tiles, acc)
            return acc

        put_end(fine, fs, lax.fori_loop(0, nx // 2, add, zero))
        send(fine, fs)
        wait(fine, fs)

        def rest(x, halo):
            c, sums, halo = around(fine, fs, x, halo)
            for j in range(nj):
                at = pl.ds(j, S, stride=nj)
                r = f_ref[x, at, :] - ((6.0 + d_ref[x, at, :]) * c[j] - sums[j])
                if cycle < CYCLES - 1:
                    fine.F[x, j] = r
                else:
                    r_ref[x, at, :] = r
            return halo

        lax.fori_loop(0, nx, rest, face_start(fine, fs))
        slot = 1 - fs


def solution(mesh):
    sizes = tuple(mesh.shape[a] for a in AXES)
    assert sizes[2] == 2

    def body(right_side, diagonal):
        nx, ny, nz = right_side.shape
        assert nz == L and ny % (2 * S) == 0 and nx % 2 == 0
        nj = ny // S
        assert nx * nj <= L
        shape = jax.ShapeDtypeStruct(right_side.shape, jnp.float32)
        vmem = pl.BlockSpec(memory_space=pltpu.VMEM)
        return pl.pallas_call(
            functools.partial(kernel, sizes, nx, nj),
            out_shape=(shape, shape),
            in_specs=[vmem, vmem],
            out_specs=(vmem, vmem),
            scratch_shapes=scratch_of(nx, nj)
            + scratch_of(nx // 2, nj // 2)
            + [pltpu.VMEM((nx, nj, S, L), jnp.float32)],
            compiler_params=pltpu.CompilerParams(
                collective_id=0, has_side_effects=True, vmem_limit_bytes=32 * 1024 * 1024
            ),
        )(right_side, diagonal)

    return jax.shard_map(
        body,
        mesh=mesh,
        in_specs=(P(*AXES), P(*AXES)),
        out_specs=(P(*AXES), P(*AXES)),
        check_vma=False,
    )
```

```python
import functools

import jax
import jax.numpy as jnp
from jax import lax
from jax.experimental import pallas as pl
from jax.experimental.pallas import tpu as pltpu
from jax.sharding import PartitionSpec as P

CYCLES = 2
SWEEPS = 5
COARSE_SWEEPS = 6
W = 2.0 / 3.0
AXES = ("gx", "gy", "sa")
MESH = pl.DeviceIdType.MESH
S = 8
L = 128
UNIT = 16


class Level:
    def __init__(self, nx, nj, dz, refs):
        self.nx, self.nj, self.dz = nx, nj, dz
        self.unit = UNIT // dz
        self.E, self.F, self.G, self.YS, self.YR, self.ZS, self.ZR, self.ssem, self.rsem = refs


def scratch_of(nx, nj):
    return [
        pltpu.VMEM((2, nx + 2, nj, S, L), jnp.float32),
        pltpu.VMEM((nx, nj, S, L), jnp.float32),
        pltpu.VMEM((nx, nj, S, L), jnp.float32),
        pltpu.VMEM((2, 2, nx, L), jnp.float32),
        pltpu.VMEM((2, 2, nx, L), jnp.float32),
        pltpu.VMEM((2, S, L), jnp.float32),
        pltpu.VMEM((2, S, L), jnp.float32),
        pltpu.SemaphoreType.DMA((2, 5)),
        pltpu.SemaphoreType.DMA((2, 5)),
    ]


def kernel(sizes, nx, nj, f_ref, d_ref, p_ref, r_ref, *scratch):
    fine = Level(nx, nj, 1, scratch[0:9])
    coarse = Level(nx // 2, nj // 2, 2, scratch[9:18])
    PB = scratch[18]
    gx, gy, sa = (lax.axis_index(a) for a in AXES)
    ngx, ngy, _ = sizes
    has = [gx > 0, gx < ngx - 1, gy > 0, gy < ngy - 1, None]
    to = [
        (gx - 1, gy, sa),
        (gx + 1, gy, sa),
        (gx, gy - 1, sa),
        (gx, gy + 1, sa),
        (gx, gy, 1 - sa),
    ]

    lane = lax.broadcasted_iota(jnp.int32, (S, L), 1)
    row = lax.broadcasted_iota(jnp.int32, (S, L), 0)
    even = lane % 2 == 0
    zero = jnp.zeros((S, L), jnp.float32)

    def when(cond, fn):
        if cond is None:
            fn()
        else:
            pl.when(cond)(fn)

    def copies(lv, slot):
        pairs = [
            (lv.E.at[slot, 1], lv.E.at[slot, lv.nx + 1]),
            (lv.E.at[slot, lv.nx], lv.E.at[slot, 0]),
            (lv.YS.at[slot, 0], lv.YR.at[slot, 1]),
            (lv.YS.at[slot, 1], lv.YR.at[slot, 0]),
            (lv.ZS.at[slot], lv.ZR.at[slot]),
        ]
        back = [1, 0, 3, 2, 4]
        return [
            pltpu.make_async_remote_copy(
                src_ref=a,
                dst_ref=b,
                send_sem=lv.ssem.at[slot, i],
                recv_sem=lv.rsem.at[slot, back[i]],
                device_id=to[i],
                device_id_type=MESH,
            )
            for i, (a, b) in enumerate(pairs)
        ]

    def arrivals(lv, slot):
        cs = copies(lv, slot)
        return [cs[1], cs[0], cs[3], cs[2], cs[4]]

    def send(lv, slot):
        cs = copies(lv, slot)
        for i in range(5):
            when(has[i], cs[i].start)

    def wait(lv, slot):
        cs = copies(lv, slot)
        ar = arrivals(lv, slot)
        for i in range(5):
            def both(i=i):
                cs[i].wait_send()
                ar[i].wait_recv()

            when(has[i], both)

    def face(lv):
        base = jnp.where(sa == 0, L - lv.dz, 0)
        return lax.rem(lane - base + L, L) // lv.dz

    def loop(count, unit, fn, carry):
        unit = min(unit, count)

        def group(g, carry):
            for i in range(unit):
                carry = fn(g * unit, i, carry)
            return carry

        if unit == count:
            return group(0, carry)
        return lax.fori_loop(0, count // unit, group, carry)

    def turn(t, by):
        by %= L
        return t if by == 0 else pltpu.roll(t, by, 1)

    def put(lv, slot, x, i, tiles, acc):
        rel = face(lv)
        for j, t in enumerate(tiles):
            lv.E[slot, x + 1, j] = t
            k = i * lv.nj + j
            acc = jnp.where(rel == k, turn(t, lv.dz * k), acc)
        lv.YS[slot, 0, pl.ds(x, 1), :] = tiles[0][0:1]
        lv.YS[slot, 1, pl.ds(x, 1), :] = tiles[-1][S - 1 : S]
        return turn(acc, -lv.dz * lv.nj * lv.unit) if i == lv.unit - 1 else acc

    def put_end(lv, slot, acc):
        lv.ZS[slot] = turn(acc, lv.nx * lv.nj * lv.dz)

    def face_start(lv, slot):
        z = lv.ZR[slot]
        return jnp.where(sa == 0, pltpu.roll(z, L - lv.dz, 1), pltpu.roll(z, lv.dz, 1))

    def around(lv, slot, x, i, halo):
        nj, dz = lv.nj, lv.dz
        mine = face(lv) == 0
        c = [lv.E[slot, x + 1, j] for j in range(nj)]
        below = jnp.where(row == 0, lv.YR[slot, 0, pl.ds(x, 1), :], pltpu.roll(c[-1], 1, 0))
        above = jnp.where(row == S - 1, lv.YR[slot, 1, pl.ds(x, 1), :], pltpu.roll(c[0], S - 1, 0))
        ext = [below] + c + [above]
        sums = []
        for j in range(nj):
            t = lv.E[slot, x, j] + lv.E[slot, x + 2, j] + (ext[j] + ext[j + 2])
            zl = jnp.where(lane < dz, 0.0, pltpu.roll(c[j], dz, 1))
            zr = jnp.where(lane >= L - dz, 0.0, pltpu.roll(c[j], L - dz, 1))
            h = turn(halo, -dz * (i * nj + j))
            sums.append(t + (zl + zr) + jnp.where(mine, h, 0.0))
        if i == lv.unit - 1:
            halo = turn(halo, -dz * nj * lv.unit)
        return c, sums, halo

    def sweep(lv, src, last):
        dst = 1 - src

        def plane(first, i, carry):
            halo, acc = carry
            x = first + i
            c, sums, halo = around(lv, src, x, i, halo)
            new = [
                (1.0 - W) * c[j] + lv.G[x, j] * (lv.F[x, j] + sums[j]) for j in range(lv.nj)
            ]
            if last:
                for j in range(lv.nj):
                    lv.E[dst, x + 1, j] = new[j]
            else:
                acc = put(lv, dst, x, i, new, acc)
            return halo, acc

        _, acc = loop(lv.nx, lv.unit, plane, (face_start(lv, src), zero))
        if not last:
            put_end(lv, dst, acc)

    def restrict(tiles):
        t = (tiles[0] + tiles[1]) + (tiles[2] + tiles[3])
        return 0.5 * (t + jnp.where(even, pltpu.roll(t, L - 1, 1), pltpu.roll(t, 1, 1)))

    def begin(slot, first):
        def plane(start, I, carry):
            facc, cacc = carry
            X = start + I
            f = [[None] * nj, [None] * nj]
            d = [[None] * nj, [None] * nj]
            for i in range(2):
                x = 2 * X + i
                for j in range(nj):
                    if first:
                        f[i][j] = f_ref[x, pl.ds(j, S, stride=nj), :]
                        fine.F[x, j] = f[i][j]
                        d[i][j] = d_ref[x, pl.ds(j, S, stride=nj), :]
                        fine.G[x, j] = W / (6.0 + d[i][j])
                    else:
                        f[i][j] = fine.F[x, j]
                new = [fine.G[x, j] * f[i][j] for j in range(nj)]
                facc = put(fine, slot, x, 2 * I + i, new, facc)
            new = []
            for J in range(nj // 2):
                cf = restrict([f[i][2 * J + k] for i in range(2) for k in range(2)])
                coarse.F[X, J] = cf
                if first:
                    cd = restrict([d[i][2 * J + k] for i in range(2) for k in range(2)])
                    coarse.G[X, J] = W / (6.0 + cd)
                new.append(coarse.G[X, J] * cf)
            return facc, put(coarse, slot, X, I, new, cacc)

        facc, cacc = loop(nx // 2, coarse.unit, plane, (zero, zero))
        put_end(fine, slot, facc)
        put_end(coarse, slot, cacc)

    for lv in (fine, coarse):
        for slot in range(2):
            for plane in (0, lv.nx + 1):
                lv.E[slot, plane] = jnp.zeros((lv.nj, S, L), jnp.float32)
            lv.YR[slot] = jnp.zeros((2, lv.nx, L), jnp.float32)

    barrier = pltpu.get_barrier_semaphore()
    for i in range(5):
        def hello(i=i):
            pl.semaphore_signal(barrier, inc=1, device_id=to[i], device_id_type=MESH)

        when(has[i], hello)
    count = 1 + sum(h.astype(jnp.int32) for h in has[:4])
    pl.semaphore_wait(barrier, count)

    slot = 0
    for cycle in range(CYCLES):
        begin(slot, cycle == 0)
        send(fine, slot)
        send(coarse, slot)
        fs = cs = slot
        for step in range(max(SWEEPS, COARSE_SWEEPS) - 1):
            if step < SWEEPS - 1:
                last = step == SWEEPS - 2
                wait(fine, fs)
                sweep(fine, fs, last)
                fs = 1 - fs
                if not last:
                    send(fine, fs)
            if step < COARSE_SWEEPS - 1:
                last = step == COARSE_SWEEPS - 2
                wait(coarse, cs)
                sweep(coarse, cs, last)
                cs = 1 - cs
                if not last:
                    send(coarse, cs)

        def add(start, I, acc):
            X = start + I
            for i in range(2):
                x = 2 * X + i
                tiles = []
                for j in range(nj):
                    t = fine.E[fs, x + 1, j] + coarse.E[cs, X + 1, j // 2]
                    if cycle > 0:
                        t = t + PB[x, j]
                    if cycle < CYCLES - 1:
                        PB[x, j] = t
                    else:
                        p_ref[x, pl.ds(j, S, stride=nj), :] = t
                    tiles.append(t)
                acc = put(fine, fs, x, 2 * I + i, tiles, acc)
            return acc

        put_end(fine, fs, loop(nx // 2, coarse.unit, add, zero))
        send(fine, fs)
        wait(fine, fs)

        def rest(first, i, halo):
            x = first + i
            c, sums, halo = around(fine, fs, x, i, halo)
            for j in range(nj):
                at = pl.ds(j, S, stride=nj)
                r = f_ref[x, at, :] - ((6.0 + d_ref[x, at, :]) * c[j] - sums[j])
                if cycle < CYCLES - 1:
                    fine.F[x, j] = r
                else:
                    r_ref[x, at, :] = r
            return halo

        loop(nx, fine.unit, rest, face_start(fine, fs))
        slot = 1 - fs


def solution(mesh):
    sizes = tuple(mesh.shape[a] for a in AXES)
    assert sizes[2] == 2

    def body(right_side, diagonal):
        nx, ny, nz = right_side.shape
        assert nz == L and ny % (2 * S) == 0 and nx % 2 == 0
        nj = ny // S
        assert nx * nj <= L
        shape = jax.ShapeDtypeStruct(right_side.shape, jnp.float32)
        vmem = pl.BlockSpec(memory_space=pltpu.VMEM)
        return pl.pallas_call(
            functools.partial(kernel, sizes, nx, nj),
            out_shape=(shape, shape),
            in_specs=[vmem, vmem],
            out_specs=(vmem, vmem),
            scratch_shapes=scratch_of(nx, nj)
            + scratch_of(nx // 2, nj // 2)
            + [pltpu.VMEM((nx, nj, S, L), jnp.float32)],
            compiler_params=pltpu.CompilerParams(
                collective_id=0, has_side_effects=True, vmem_limit_bytes=32 * 1024 * 1024
            ),
        )(right_side, diagonal)

    return jax.shard_map(
        body,
        mesh=mesh,
        in_specs=(P(*AXES), P(*AXES)),
        out_specs=(P(*AXES), P(*AXES)),
        check_vma=False,
    )
```

```python
import functools

import jax
import jax.numpy as jnp
from jax import lax
from jax.experimental import pallas as pl
from jax.experimental.pallas import tpu as pltpu
from jax.sharding import PartitionSpec as P

CYCLES = 2
SWEEPS = 5
COARSE_SWEEPS = 6
W = 2.0 / 3.0
AXES = ("gx", "gy", "sa")
MESH = pl.DeviceIdType.MESH
S = 8
L = 128
UNIT = 16


class Level:
    def __init__(self, nx, nj, dz, refs):
        self.nx, self.nj, self.dz = nx, nj, dz
        self.unit = UNIT // dz
        self.sent = [False, False]
        self.E, self.F, self.G, self.YS, self.YR, self.ZS, self.ZR, self.ssem, self.rsem = refs


def scratch_of(nx, nj):
    return [
        pltpu.VMEM((2, nx + 2, nj, S, L), jnp.float32),
        pltpu.VMEM((nx, nj, S, L), jnp.float32),
        pltpu.VMEM((nx, nj, S, L), jnp.float32),
        pltpu.VMEM((2, 2, nx, L), jnp.float32),
        pltpu.VMEM((2, 2, nx, L), jnp.float32),
        pltpu.VMEM((2, S, L), jnp.float32),
        pltpu.VMEM((2, S, L), jnp.float32),
        pltpu.SemaphoreType.DMA((2, 5)),
        pltpu.SemaphoreType.DMA((2, 5)),
    ]


def kernel(sizes, nx, nj, f_hbm, d_hbm, p_ref, r_ref, *scratch):
    fine = Level(nx, nj, 1, scratch[0:9])
    coarse = Level(nx // 2, nj // 2, 2, scratch[9:18])
    PB, f_ref, d_ref, isem = scratch[18:]
    loads = [
        pltpu.make_async_copy(f_hbm, f_ref, isem.at[0]),
        pltpu.make_async_copy(d_hbm, d_ref, isem.at[1]),
    ]
    for load in loads:
        load.start()
    gx, gy, sa = (lax.axis_index(a) for a in AXES)
    ngx, ngy, _ = sizes
    has = [gx > 0, gx < ngx - 1, gy > 0, gy < ngy - 1, None]
    to = [
        (gx - 1, gy, sa),
        (gx + 1, gy, sa),
        (gx, gy - 1, sa),
        (gx, gy + 1, sa),
        (gx, gy, 1 - sa),
    ]

    lane = lax.broadcasted_iota(jnp.int32, (S, L), 1)
    row = lax.broadcasted_iota(jnp.int32, (S, L), 0)
    even = lane % 2 == 0
    zero = jnp.zeros((S, L), jnp.float32)

    def when(cond, fn):
        if cond is None:
            fn()
        else:
            pl.when(cond)(fn)

    def copies(lv, slot):
        pairs = [
            (lv.E.at[slot, 1], lv.E.at[slot, lv.nx + 1]),
            (lv.E.at[slot, lv.nx], lv.E.at[slot, 0]),
            (lv.YS.at[slot, 0], lv.YR.at[slot, 1]),
            (lv.YS.at[slot, 1], lv.YR.at[slot, 0]),
            (lv.ZS.at[slot], lv.ZR.at[slot]),
        ]
        back = [1, 0, 3, 2, 4]
        return [
            pltpu.make_async_remote_copy(
                src_ref=a,
                dst_ref=b,
                send_sem=lv.ssem.at[slot, i],
                recv_sem=lv.rsem.at[slot, back[i]],
                device_id=to[i],
                device_id_type=MESH,
            )
            for i, (a, b) in enumerate(pairs)
        ]

    def arrivals(lv, slot):
        cs = copies(lv, slot)
        return [cs[1], cs[0], cs[3], cs[2], cs[4]]

    def send(lv, slot):
        cs = copies(lv, slot)
        for i in range(5):
            when(has[i], cs[i].start)
        lv.sent[slot] = True

    def free(lv, slot):
        if lv.sent[slot]:
            cs = copies(lv, slot)
            for i in range(5):
                when(has[i], cs[i].wait_send)
            lv.sent[slot] = False

    def wait(lv, slot):
        ar = arrivals(lv, slot)
        for i in range(5):
            when(has[i], ar[i].wait_recv)
        free(lv, 1 - slot)

    def face(lv):
        base = jnp.where(sa == 0, L - lv.dz, 0)
        return lax.rem(lane - base + L, L) // lv.dz

    def loop(count, unit, fn, carry):
        unit = min(unit, count)

        def group(g, carry):
            for i in range(unit):
                carry = fn(g * unit, i, carry)
            return carry

        if unit == count:
            return group(0, carry)
        return lax.fori_loop(0, count // unit, group, carry)

    def turn(t, by):
        by %= L
        return t if by == 0 else pltpu.roll(t, by, 1)

    def put(lv, slot, x, i, tiles, acc):
        rel = face(lv)
        for j, t in enumerate(tiles):
            lv.E[slot, x + 1, j] = t
            k = i * lv.nj + j
            acc = jnp.where(rel == k, turn(t, lv.dz * k), acc)
        lv.YS[slot, 0, pl.ds(x, 1), :] = tiles[0][0:1]
        lv.YS[slot, 1, pl.ds(x, 1), :] = tiles[-1][S - 1 : S]
        return turn(acc, -lv.dz * lv.nj * lv.unit) if i == lv.unit - 1 else acc

    def put_end(lv, slot, acc):
        lv.ZS[slot] = turn(acc, lv.nx * lv.nj * lv.dz)

    def face_start(lv, slot):
        z = lv.ZR[slot]
        return jnp.where(sa == 0, pltpu.roll(z, L - lv.dz, 1), pltpu.roll(z, lv.dz, 1))

    def around(lv, slot, x, i, halo):
        nj, dz = lv.nj, lv.dz
        mine = face(lv) == 0
        c = [lv.E[slot, x + 1, j] for j in range(nj)]
        below = jnp.where(row == 0, lv.YR[slot, 0, pl.ds(x, 1), :], pltpu.roll(c[-1], 1, 0))
        above = jnp.where(row == S - 1, lv.YR[slot, 1, pl.ds(x, 1), :], pltpu.roll(c[0], S - 1, 0))
        ext = [below] + c + [above]
        sums = []
        for j in range(nj):
            t = lv.E[slot, x, j] + lv.E[slot, x + 2, j] + (ext[j] + ext[j + 2])
            zl = jnp.where(lane < dz, 0.0, pltpu.roll(c[j], dz, 1))
            zr = jnp.where(lane >= L - dz, 0.0, pltpu.roll(c[j], L - dz, 1))
            h = turn(halo, -dz * (i * nj + j))
            sums.append(t + (zl + zr) + jnp.where(mine, h, 0.0))
        if i == lv.unit - 1:
            halo = turn(halo, -dz * nj * lv.unit)
        return c, sums, halo

    def sweep(lv, src, last):
        dst = 1 - src

        def plane(first, i, carry):
            halo, acc = carry
            x = first + i
            c, sums, halo = around(lv, src, x, i, halo)
            new = [
                (1.0 - W) * c[j] + lv.G[x, j] * (lv.F[x, j] + sums[j]) for j in range(lv.nj)
            ]
            if last:
                for j in range(lv.nj):
                    lv.E[dst, x + 1, j] = new[j]
            else:
                acc = put(lv, dst, x, i, new, acc)
            return halo, acc

        _, acc = loop(lv.nx, lv.unit, plane, (face_start(lv, src), zero))
        if not last:
            put_end(lv, dst, acc)

    def restrict(tiles):
        t = (tiles[0] + tiles[1]) + (tiles[2] + tiles[3])
        return 0.5 * (t + jnp.where(even, pltpu.roll(t, L - 1, 1), pltpu.roll(t, 1, 1)))

    def begin(slot, first):
        def low(start, I, acc):
            X = start + I
            new = []
            for J in range(nj // 2):
                cells = [(2 * X + i, 2 * J + k) for i in range(2) for k in range(2)]
                if first:
                    at = [(x, pl.ds(j, S, stride=nj)) for x, j in cells]
                    cf = restrict([f_ref[x, y, :] for x, y in at])
                    cd = restrict([d_ref[x, y, :] for x, y in at])
                    coarse.G[X, J] = W / (6.0 + cd)
                else:
                    cf = restrict([fine.F[x, j] for x, j in cells])
                coarse.F[X, J] = cf
                new.append(coarse.G[X, J] * cf)
            return put(coarse, slot, X, I, new, acc)

        put_end(coarse, slot, loop(nx // 2, coarse.unit, low, zero))
        if first:
            pl.semaphore_wait(barrier, count)
        send(coarse, slot)

        def high(start, i, acc):
            x = start + i
            new = []
            for j in range(nj):
                if first:
                    y = pl.ds(j, S, stride=nj)
                    f = f_ref[x, y, :]
                    g = W / (6.0 + d_ref[x, y, :])
                    fine.F[x, j] = f
                    fine.G[x, j] = g
                else:
                    f = fine.F[x, j]
                    g = fine.G[x, j]
                new.append(g * f)
            return put(fine, slot, x, i, new, acc)

        put_end(fine, slot, loop(nx, fine.unit, high, zero))
        send(fine, slot)

    for lv in (fine, coarse):
        for slot in range(2):
            for plane in (0, lv.nx + 1):
                lv.E[slot, plane] = jnp.zeros((lv.nj, S, L), jnp.float32)
            lv.YR[slot] = jnp.zeros((2, lv.nx, L), jnp.float32)

    barrier = pltpu.get_barrier_semaphore()
    for i in range(5):
        def hello(i=i):
            pl.semaphore_signal(barrier, inc=1, device_id=to[i], device_id_type=MESH)

        when(has[i], hello)
    count = 1 + sum(h.astype(jnp.int32) for h in has[:4])
    for load in loads:
        load.wait()

    slot = 0
    for cycle in range(CYCLES):
        begin(slot, cycle == 0)
        fs = cs = slot
        for step in range(max(SWEEPS, COARSE_SWEEPS) - 1):
            if step < COARSE_SWEEPS - 1:
                last = step == COARSE_SWEEPS - 2
                wait(coarse, cs)
                sweep(coarse, cs, last)
                cs = 1 - cs
                if not last:
                    send(coarse, cs)
            if step < SWEEPS - 1:
                last = step == SWEEPS - 2
                wait(fine, fs)
                sweep(fine, fs, last)
                fs = 1 - fs
                if not last:
                    send(fine, fs)

        def add(start, I, acc):
            X = start + I
            for i in range(2):
                x = 2 * X + i
                tiles = []
                for j in range(nj):
                    t = fine.E[fs, x + 1, j] + coarse.E[cs, X + 1, j // 2]
                    if cycle > 0:
                        t = t + PB[x, j]
                    if cycle < CYCLES - 1:
                        PB[x, j] = t
                    else:
                        p_ref[x, pl.ds(j, S, stride=nj), :] = t
                    tiles.append(t)
                acc = put(fine, fs, x, 2 * I + i, tiles, acc)
            return acc

        put_end(fine, fs, loop(nx // 2, coarse.unit, add, zero))
        send(fine, fs)
        wait(fine, fs)

        def rest(first, i, halo):
            x = first + i
            c, sums, halo = around(fine, fs, x, i, halo)
            for j in range(nj):
                at = pl.ds(j, S, stride=nj)
                r = f_ref[x, at, :] - ((6.0 + d_ref[x, at, :]) * c[j] - sums[j])
                if cycle < CYCLES - 1:
                    fine.F[x, j] = r
                else:
                    r_ref[x, at, :] = r
            return halo

        loop(nx, fine.unit, rest, face_start(fine, fs))
        slot = 1 - fs
        free(fine, slot)
        free(coarse, slot)
    for lv in (fine, coarse):
        for at in range(2):
            free(lv, at)


def solution(mesh):
    sizes = tuple(mesh.shape[a] for a in AXES)
    assert sizes[2] == 2

    def body(right_side, diagonal):
        nx, ny, nz = right_side.shape
        assert nz == L and ny % (2 * S) == 0 and nx % 2 == 0
        nj = ny // S
        assert nx * nj <= L
        shape = jax.ShapeDtypeStruct(right_side.shape, jnp.float32)
        vmem = pl.BlockSpec(memory_space=pltpu.VMEM)
        hbm = pl.BlockSpec(memory_space=pltpu.HBM)
        return pl.pallas_call(
            functools.partial(kernel, sizes, nx, nj),
            out_shape=(shape, shape),
            in_specs=[hbm, hbm],
            out_specs=(vmem, vmem),
            scratch_shapes=scratch_of(nx, nj)
            + scratch_of(nx // 2, nj // 2)
            + [
                pltpu.VMEM((nx, nj, S, L), jnp.float32),
                pltpu.VMEM(right_side.shape, jnp.float32),
                pltpu.VMEM(right_side.shape, jnp.float32),
                pltpu.SemaphoreType.DMA((2,)),
            ],
            compiler_params=pltpu.CompilerParams(
                collective_id=0, has_side_effects=True, vmem_limit_bytes=32 * 1024 * 1024
            ),
        )(right_side, diagonal)

    return jax.shard_map(
        body,
        mesh=mesh,
        in_specs=(P(*AXES), P(*AXES)),
        out_specs=(P(*AXES), P(*AXES)),
        check_vma=False,
    )
```

```python
import functools

import jax
import jax.numpy as jnp
from jax import lax
from jax.experimental import pallas as pl
from jax.experimental.pallas import tpu as pltpu
from jax.sharding import PartitionSpec as P

CYCLES = 2
SWEEPS = 5
COARSE_SWEEPS = 6
W = 2.0 / 3.0
AXES = ("gx", "gy", "sa")
MESH = pl.DeviceIdType.MESH
S = 8
L = 128
UNIT = 16


class Level:
    def __init__(self, nx, nj, dz, refs):
        self.nx, self.nj, self.dz = nx, nj, dz
        self.unit = UNIT // dz
        self.sent = [False, False]
        self.E, self.F, self.G, self.YS, self.YR, self.ZS, self.ZR, self.ssem, self.rsem = refs


def scratch_of(nx, nj):
    return [
        pltpu.VMEM((2, nx + 2, nj, S, L), jnp.float32),
        pltpu.VMEM((nx, nj, S, L), jnp.float32),
        pltpu.VMEM((nx, nj, S, L), jnp.float32),
        pltpu.VMEM((2, 2, nx, L), jnp.float32),
        pltpu.VMEM((2, 2, nx, L), jnp.float32),
        pltpu.VMEM((2, S, L), jnp.float32),
        pltpu.VMEM((2, S, L), jnp.float32),
        pltpu.SemaphoreType.DMA((2, 5)),
        pltpu.SemaphoreType.DMA((2, 5)),
    ]


def kernel(sizes, nx, nj, f_hbm, d_hbm, p_ref, r_ref, *scratch):
    fine = Level(nx, nj, 1, scratch[0:9])
    coarse = Level(nx // 2, nj // 2, 2, scratch[9:18])
    PB, f_ref, d_ref, isem = scratch[18:]
    loads = [
        pltpu.make_async_copy(f_hbm, f_ref, isem.at[0]),
        pltpu.make_async_copy(d_hbm, d_ref, isem.at[1]),
    ]
    for load in loads:
        load.start()
    gx, gy, sa = (lax.axis_index(a) for a in AXES)
    ngx, ngy, _ = sizes
    has = [gx > 0, gx < ngx - 1, gy > 0, gy < ngy - 1, None]
    to = [
        (gx - 1, gy, sa),
        (gx + 1, gy, sa),
        (gx, gy - 1, sa),
        (gx, gy + 1, sa),
        (gx, gy, 1 - sa),
    ]

    lane = lax.broadcasted_iota(jnp.int32, (S, L), 1)
    row = lax.broadcasted_iota(jnp.int32, (S, L), 0)
    even = lane % 2 == 0
    zero = jnp.zeros((S, L), jnp.float32)

    def when(cond, fn):
        if cond is None:
            fn()
        else:
            pl.when(cond)(fn)

    def copies(lv, slot):
        pairs = [
            (lv.E.at[slot, 1], lv.E.at[slot, lv.nx + 1]),
            (lv.E.at[slot, lv.nx], lv.E.at[slot, 0]),
            (lv.YS.at[slot, 0], lv.YR.at[slot, 1]),
            (lv.YS.at[slot, 1], lv.YR.at[slot, 0]),
            (lv.ZS.at[slot], lv.ZR.at[slot]),
        ]
        back = [1, 0, 3, 2, 4]
        return [
            pltpu.make_async_remote_copy(
                src_ref=a,
                dst_ref=b,
                send_sem=lv.ssem.at[slot, i],
                recv_sem=lv.rsem.at[slot, back[i]],
                device_id=to[i],
                device_id_type=MESH,
            )
            for i, (a, b) in enumerate(pairs)
        ]

    def arrivals(lv, slot):
        cs = copies(lv, slot)
        return [cs[1], cs[0], cs[3], cs[2], cs[4]]

    def send(lv, slot, dirs=(2, 3, 4)):
        cs = copies(lv, slot)
        for i in dirs:
            when(has[i], cs[i].start)
        lv.sent[slot] = True

    def free(lv, slot):
        if lv.sent[slot]:
            cs = copies(lv, slot)
            for i in range(5):
                when(has[i], cs[i].wait_send)
            lv.sent[slot] = False

    def wait(lv, slot):
        ar = arrivals(lv, slot)
        for i in range(5):
            when(has[i], ar[i].wait_recv)
        free(lv, 1 - slot)

    def face(lv):
        base = jnp.where(sa == 0, L - lv.dz, 0)
        return lax.rem(lane - base + L, L) // lv.dz

    def loop(count, unit, fn, carry, early=None):
        unit = min(unit, count)

        def group(g, carry):
            for i in range(unit):
                carry = fn(g * unit, i, carry)
            return carry

        if unit == count:
            for n, i in enumerate([0, count - 1, *range(1, count - 1)]):
                carry = fn(0, i, carry)
                if n == 1 and early is not None:
                    early()
            return carry
        assert early is None
        return lax.fori_loop(0, count // unit, group, carry)

    def turn(t, by):
        by %= L
        return t if by == 0 else pltpu.roll(t, by, 1)

    def put(lv, slot, x, i, tiles, acc):
        rel = face(lv)
        for j, t in enumerate(tiles):
            lv.E[slot, x + 1, j] = t
            k = i * lv.nj + j
            acc = jnp.where(rel == k, turn(t, lv.dz * k), acc)
        lv.YS[slot, 0, pl.ds(x, 1), :] = tiles[0][0:1]
        lv.YS[slot, 1, pl.ds(x, 1), :] = tiles[-1][S - 1 : S]
        return turn(acc, -lv.dz * lv.nj * lv.unit) if i == lv.unit - 1 < lv.nx - 1 else acc

    def put_end(lv, slot, acc):
        lv.ZS[slot] = turn(acc, lv.nx * lv.nj * lv.dz if lv.unit < lv.nx else 0)

    def face_start(lv, slot):
        z = lv.ZR[slot]
        return jnp.where(sa == 0, pltpu.roll(z, L - lv.dz, 1), pltpu.roll(z, lv.dz, 1))

    def around(lv, slot, x, i, halo):
        nj, dz = lv.nj, lv.dz
        mine = face(lv) == 0
        c = [lv.E[slot, x + 1, j] for j in range(nj)]
        below = jnp.where(row == 0, lv.YR[slot, 0, pl.ds(x, 1), :], pltpu.roll(c[-1], 1, 0))
        above = jnp.where(row == S - 1, lv.YR[slot, 1, pl.ds(x, 1), :], pltpu.roll(c[0], S - 1, 0))
        ext = [below] + c + [above]
        sums = []
        for j in range(nj):
            t = lv.E[slot, x, j] + lv.E[slot, x + 2, j] + (ext[j] + ext[j + 2])
            zl = jnp.where(lane < dz, 0.0, pltpu.roll(c[j], dz, 1))
            zr = jnp.where(lane >= L - dz, 0.0, pltpu.roll(c[j], L - dz, 1))
            h = turn(halo, -dz * (i * nj + j))
            sums.append(t + (zl + zr) + jnp.where(mine, h, 0.0))
        if i == lv.unit - 1 < lv.nx - 1:
            halo = turn(halo, -dz * nj * lv.unit)
        return c, sums, halo

    def sweep(lv, src, last):
        dst = 1 - src

        def plane(first, i, carry):
            halo, acc = carry
            x = first + i
            c, sums, halo = around(lv, src, x, i, halo)
            new = [
                (1.0 - W) * c[j] + lv.G[x, j] * (lv.F[x, j] + sums[j]) for j in range(lv.nj)
            ]
            if last:
                for j in range(lv.nj):
                    lv.E[dst, x + 1, j] = new[j]
            else:
                acc = put(lv, dst, x, i, new, acc)
            return halo, acc

        early = None if last else lambda: send(lv, dst, (0, 1))
        _, acc = loop(lv.nx, lv.unit, plane, (face_start(lv, src), zero), early)
        if not last:
            put_end(lv, dst, acc)

    def restrict(tiles):
        t = (tiles[0] + tiles[1]) + (tiles[2] + tiles[3])
        return 0.5 * (t + jnp.where(even, pltpu.roll(t, L - 1, 1), pltpu.roll(t, 1, 1)))

    def begin(slot, first):
        def low(start, I, acc):
            X = start + I
            new = []
            for J in range(nj // 2):
                cells = [(2 * X + i, 2 * J + k) for i in range(2) for k in range(2)]
                if first:
                    at = [(x, pl.ds(j, S, stride=nj)) for x, j in cells]
                    cf = restrict([f_ref[x, y, :] for x, y in at])
                    cd = restrict([d_ref[x, y, :] for x, y in at])
                    coarse.G[X, J] = W / (6.0 + cd)
                else:
                    cf = restrict([fine.F[x, j] for x, j in cells])
                coarse.F[X, J] = cf
                new.append(coarse.G[X, J] * cf)
            return put(coarse, slot, X, I, new, acc)

        put_end(coarse, slot, loop(nx // 2, coarse.unit, low, zero))
        if first:
            pl.semaphore_wait(barrier, count)
        send(coarse, slot, range(5))

        def high(start, i, acc):
            x = start + i
            new = []
            for j in range(nj):
                if first:
                    y = pl.ds(j, S, stride=nj)
                    f = f_ref[x, y, :]
                    g = W / (6.0 + d_ref[x, y, :])
                    fine.F[x, j] = f
                    fine.G[x, j] = g
                else:
                    f = fine.F[x, j]
                    g = fine.G[x, j]
                new.append(g * f)
            return put(fine, slot, x, i, new, acc)

        put_end(fine, slot, loop(nx, fine.unit, high, zero))
        send(fine, slot, range(5))

    for lv in (fine, coarse):
        for slot in range(2):
            for plane in (0, lv.nx + 1):
                lv.E[slot, plane] = jnp.zeros((lv.nj, S, L), jnp.float32)
            lv.YR[slot] = jnp.zeros((2, lv.nx, L), jnp.float32)

    barrier = pltpu.get_barrier_semaphore()
    for i in range(5):
        def hello(i=i):
            pl.semaphore_signal(barrier, inc=1, device_id=to[i], device_id_type=MESH)

        when(has[i], hello)
    count = 1 + sum(h.astype(jnp.int32) for h in has[:4])
    for load in loads:
        load.wait()

    slot = 0
    for cycle in range(CYCLES):
        begin(slot, cycle == 0)
        fs = cs = slot
        for step in range(max(SWEEPS, COARSE_SWEEPS) - 1):
            if step < COARSE_SWEEPS - 1:
                last = step == COARSE_SWEEPS - 2
                wait(coarse, cs)
                sweep(coarse, cs, last)
                cs = 1 - cs
                if not last:
                    send(coarse, cs)
            if step < SWEEPS - 1:
                last = step == SWEEPS - 2
                wait(fine, fs)
                sweep(fine, fs, last)
                fs = 1 - fs
                if not last:
                    send(fine, fs)

        def add(start, I, acc):
            X = start + I
            for i in range(2):
                x = 2 * X + i
                tiles = []
                for j in range(nj):
                    t = fine.E[fs, x + 1, j] + coarse.E[cs, X + 1, j // 2]
                    if cycle > 0:
                        t = t + PB[x, j]
                    if cycle < CYCLES - 1:
                        PB[x, j] = t
                    else:
                        p_ref[x, pl.ds(j, S, stride=nj), :] = t
                    tiles.append(t)
                acc = put(fine, fs, x, 2 * I + i, tiles, acc)
            return acc

        put_end(fine, fs, loop(nx // 2, coarse.unit, add, zero, lambda: send(fine, fs, (0, 1))))
        send(fine, fs)
        wait(fine, fs)

        def rest(first, i, halo):
            x = first + i
            c, sums, halo = around(fine, fs, x, i, halo)
            for j in range(nj):
                at = pl.ds(j, S, stride=nj)
                r = f_ref[x, at, :] - ((6.0 + d_ref[x, at, :]) * c[j] - sums[j])
                if cycle < CYCLES - 1:
                    fine.F[x, j] = r
                else:
                    r_ref[x, at, :] = r
            return halo

        loop(nx, fine.unit, rest, face_start(fine, fs))
        slot = 1 - fs
        free(fine, slot)
        free(coarse, slot)
    for lv in (fine, coarse):
        for at in range(2):
            free(lv, at)


def solution(mesh):
    sizes = tuple(mesh.shape[a] for a in AXES)
    assert sizes[2] == 2

    def body(right_side, diagonal):
        nx, ny, nz = right_side.shape
        assert nz == L and ny % (2 * S) == 0 and nx % 2 == 0
        nj = ny // S
        assert nx * nj <= L
        shape = jax.ShapeDtypeStruct(right_side.shape, jnp.float32)
        vmem = pl.BlockSpec(memory_space=pltpu.VMEM)
        hbm = pl.BlockSpec(memory_space=pltpu.HBM)
        return pl.pallas_call(
            functools.partial(kernel, sizes, nx, nj),
            out_shape=(shape, shape),
            in_specs=[hbm, hbm],
            out_specs=(vmem, vmem),
            scratch_shapes=scratch_of(nx, nj)
            + scratch_of(nx // 2, nj // 2)
            + [
                pltpu.VMEM((nx, nj, S, L), jnp.float32),
                pltpu.VMEM(right_side.shape, jnp.float32),
                pltpu.VMEM(right_side.shape, jnp.float32),
                pltpu.SemaphoreType.DMA((2,)),
            ],
            compiler_params=pltpu.CompilerParams(
                collective_id=0, has_side_effects=True, vmem_limit_bytes=32 * 1024 * 1024
            ),
        )(right_side, diagonal)

    return jax.shard_map(
        body,
        mesh=mesh,
        in_specs=(P(*AXES), P(*AXES)),
        out_specs=(P(*AXES), P(*AXES)),
        check_vma=False,
    )
```
